128 devices in a mesh: chan: 8 (over z, y_hi), win: 16 (over x, y_lo, core).
Axes of the slice: x: 4, y: 4 (y_hi: 2, y_lo: 2; y = y_hi * 2 + y_lo), z: 4, core: 2. Of those that a mesh axis runs over, the one named last changes fastest.
Arguments:
- records: bfloat16 [2048, 163840], P('chan', 'win'), may hold values from -50 to 50
- fir_taps: float32 [64], replicated, may hold values from -0.75 to 0.75
- plan: int32 [2, 8], replicated, may hold values from 0 to 7, as said below
Outputs:
- cross: float32 [64, 2, 2, 256, 2048], P('win', None, None, None, 'chan')
The draws below stay inside these ranges and needn't reach their ends.
Inputs may be any that keep to these rules, and one draw needn't show every extreme that they name: `plan`: in each round block c is paired with block c XOR k for one nonzero key k, the same k for all blocks of the round; the rounds use different keys.
All inputs are finite; a program needn't handle non-finite values.
Results may differ from the reference program's by a relative error of at most 0.02.
Values may be sent and summed in bfloat16 or wider, within the bound.
No kernel may reach another device: no remote copies, remote signals or barrier semaphores. Data moves between devices by JAX's collectives and lax.ppermute only.
A program may use at most 128 MiB of HBM per device.

```python
import math
from functools import partial
import jax
import jax.numpy as jnp
from jax import lax

CB = 256
WL = 256
F = 64
TAPS = 64
ROUNDS = 2
WIN_DEV = 40
BLOCKS = 8
NCH = 2048
WINDOWS = 640
TIME = 163840
N_WIN = 16


def draw_records(key, part):
    noise_key, scale_key = jax.random.split(jax.random.fold_in(key, 11), 2)
    gains = jnp.exp(jax.random.uniform(scale_key, (NCH, 1), jnp.float32) * math.log(10.0))
    noise = jnp.clip(jax.random.normal(noise_key, (NCH, TIME), jnp.float32), -5.0, 5.0)
    values = noise * gains
    return values.astype(jnp.bfloat16)


def draw_plan(key, part):
    first_key, second_key = jax.random.split(jax.random.fold_in(key, 29))
    first_pick = jax.random.randint(first_key, (), 1, BLOCKS, dtype=jnp.int32)
    second_pick = (first_pick - 1 + jax.random.randint(second_key, (), 1, BLOCKS - 1, dtype=jnp.int32)) % (BLOCKS - 1) + 1
    round_keys = jnp.stack([first_pick, second_pick]).astype(jnp.int32)
    block_numbers = jnp.arange(BLOCKS, dtype=jnp.int32)
    return jnp.bitwise_xor(block_numbers[None, :], round_keys[:, None]).astype(jnp.int32)


def bell_draw(stream_key, extent, width, bound, held_as=jnp.bfloat16):
    entries = jax.random.normal(stream_key, extent, jnp.float32) * width
    return jnp.minimum(jnp.maximum(entries, -bound), bound).astype(held_as)


def setup_inputs(seed: int = 0) -> dict:
    keys = jax.random.split(jax.random.key(seed), 4)
    return {
        "records": draw_records(jax.random.fold_in(keys[3], 71), 0),
        "fir_taps": bell_draw(keys[1], (TAPS,), 0.125, 0.75, jnp.float32),
        "plan": draw_plan(jax.random.fold_in(keys[3], 71), 0),
    }


def fir_matrix(fir_taps):
    inputs_at = jnp.arange(WL + TAPS - 1, dtype=jnp.int32)[:, None]
    outputs_at = jnp.arange(WL, dtype=jnp.int32)[None, :]
    tap_number = outputs_at + (TAPS - 1) - inputs_at
    inside = (tap_number >= 0) & (tap_number < TAPS)
    picked = fir_taps[jnp.clip(tap_number, 0, TAPS - 1)]
    return jnp.where(inside, picked, jnp.zeros_like(picked))

def whiten_block(block_rows, fir_taps):
    channels = block_rows.shape[0]
    samples = block_rows.astype(jnp.float32).reshape(channels, WINDOWS, WL)
    leading = jnp.zeros((channels, 1, TAPS - 1), samples.dtype)
    previous = jnp.concatenate([leading, samples[:, :-1, WL - TAPS + 1:]], axis=1)
    extended = jnp.concatenate([previous, samples], axis=2)
    filtered = jnp.einsum('cwi,in->cwn', extended, fir_matrix(fir_taps), precision=lax.Precision.HIGHEST)
    spectrum = jnp.fft.rfft(filtered, axis=-1)[:, :, 1:F + 1]
    stacked = jnp.concatenate([jnp.real(spectrum), jnp.imag(spectrum)], axis=-1).astype(jnp.float32)
    band_power = lax.optimization_barrier(jnp.mean(stacked * stacked, axis=-1, keepdims=True)) + 1e-06
    return (stacked / jnp.sqrt(band_power)).astype(jnp.bfloat16)

def arrange(whitened):
    channels, windows_here, doubled = whitened.shape
    return whitened.reshape(channels, windows_here, 2, doubled // 2).transpose(3, 0, 2, 1)

def stack_partners(partner_list):
    layers = []
    for arranged in partner_list:
        rotated = jnp.stack([-arranged[:, :, 1], arranged[:, :, 0]], axis=2)
        layers.append(jnp.stack([arranged, rotated], axis=1))
    joined = jnp.stack(layers, axis=1)
    bins_here, rounds_here, halves, channels, components, windows_here = joined.shape
    return joined.reshape(bins_here, rounds_here * halves * channels, components, windows_here)

def block_cross(block_index, whitened, plan):
    own_rows = arrange(whitened[block_index])
    partner_list = [arrange(whitened[plan[round_index, block_index]]) for round_index in range(ROUNDS)]
    partner_rows = stack_partners(partner_list)
    own_groups = own_rows.reshape(F, CB, 2, N_WIN, WIN_DEV).transpose(3, 0, 1, 2, 4).reshape(N_WIN, F, CB, 2 * WIN_DEV)
    partner_groups = partner_rows.reshape(F, ROUNDS * 2 * CB, 2, N_WIN, WIN_DEV).transpose(3, 0, 1, 2, 4).reshape(N_WIN, F, ROUNDS * 2 * CB, 2 * WIN_DEV)
    scale = 1.0 / math.sqrt(WINDOWS)

    def add_group(running, pieces):
        own_piece, partner_piece = pieces
        product = jnp.einsum('fjk,fak->fja', partner_piece.astype(jnp.float32), own_piece.astype(jnp.float32)) * scale
        rounded = lax.optimization_barrier(product.astype(jnp.bfloat16))
        return (running + rounded.astype(jnp.float32), None)
    start_sum = jnp.zeros((F, ROUNDS * 2 * CB, CB), jnp.float32)
    summed, ignored = lax.scan(add_group, start_sum, (own_groups, partner_groups))
    return summed

def reference(records, fir_taps, plan):
    blocks_in = records.reshape(BLOCKS, CB, TIME)
    whitened = lax.map(partial(whiten_block, fir_taps=fir_taps), blocks_in)
    per_block = lax.map(partial(block_cross, whitened=whitened, plan=plan), jnp.arange(BLOCKS, dtype=jnp.int32))
    shaped = per_block.reshape(BLOCKS, F, ROUNDS, 2, CB, CB).transpose(1, 2, 3, 4, 0, 5)
    return shaped.reshape(F, ROUNDS, 2, CB, NCH)
```

```python
import functools
import math

import jax
import jax.numpy as jnp
import numpy as np
from jax import lax
from jax.experimental import pallas as pl
from jax.experimental.pallas import tpu as pltpu
from jax.sharding import Mesh
from jax.sharding import PartitionSpec as P

WL = 256
F = 64
TAPS = 64
ROUNDS = 2
STEP_WINDOWS = 8
PIECES = 3
ROWS = 80
TILE = 16
VMEM = 48 * 1024 * 1024


def dft_rows(chips, blocks):
    place = np.arange(F)
    bin_number = blocks * (place % chips) + place // chips + 1
    phase = np.arange(WL)[None, :] * bin_number[:, None] % WL * (2.0 * math.pi / WL)
    return np.concatenate([np.cos(phase), -np.sin(phase)]).astype(np.float32)


def in_pieces(table):
    pieces = []
    rest = table
    for _ in range(PIECES):
        piece = rest.astype(jnp.bfloat16)
        pieces.append(piece)
        rest = rest - piece.astype(jnp.float32)
    return jnp.concatenate(pieces, axis=0)


def table_kernel(taps_ref, dft_ref, table_ref):
    lane = lax.broadcasted_iota(jnp.int32, (1, 2 * WL), 1)
    reversed_taps = jnp.zeros((1, 2 * WL), jnp.float32)
    for tap in range(TAPS):
        reversed_taps = jnp.where(lane == TAPS - 1 - tap, taps_ref[tap], reversed_taps)
    spread = jnp.broadcast_to(reversed_taps, (WL, 2 * WL))
    toeplitz = pltpu.roll(spread, WL - TAPS + 1, 1, stride=1, stride_axis=0)
    combined = jnp.dot(
        dft_ref[...], toeplitz, precision=lax.Precision.HIGHEST, preferred_element_type=jnp.float32
    )
    count = PIECES * 2 * F
    table_ref[:count, :] = in_pieces(combined[:, WL:])
    table_ref[count:, :] = in_pieces(combined[:, :WL])


def make_table(fir_taps, dft):
    return pl.pallas_call(
        table_kernel,
        out_shape=jax.ShapeDtypeStruct((2 * PIECES * 2 * F, WL), jnp.bfloat16),
        in_specs=[pl.BlockSpec(memory_space=pltpu.SMEM), pl.BlockSpec(memory_space=pltpu.VMEM)],
        out_specs=pl.BlockSpec(memory_space=pltpu.VMEM),
        compiler_params=pltpu.CompilerParams(vmem_limit_bytes=VMEM),
        name="table",
    )(fir_taps, dft)


def add_pieces(rows):
    count = 2 * F
    total = rows[(PIECES - 1) * count : PIECES * count]
    for piece in range(PIECES - 2, -1, -1):
        total = total + rows[piece * count : (piece + 1) * count]
    return total


NT = (((1,), (1,)), ((), ()))


def spectra_kernel(tail_ref, table_ref, records_ref, out_ref, carry_ref, held_ref):
    step = pl.program_id(0)
    count = PIECES * 2 * F

    @pl.when(step == 0)
    def _():
        rows = lax.dot_general(
            table_ref[count:, WL // 2 :], tail_ref[...], NT, preferred_element_type=jnp.float32
        )
        carry_ref[...] = add_pieces(rows)

    carry = carry_ref[...]
    for inner in range(STEP_WINDOWS):
        window = step * STEP_WINDOWS + inner
        samples = records_ref[:, inner * WL : (inner + 1) * WL]
        rows = lax.dot_general(table_ref[...], samples, NT, preferred_element_type=jnp.float32)
        stacked = add_pieces(rows[:count]) + carry
        carry = add_pieces(rows[count:])
        power = jnp.sum(stacked * stacked, axis=0, keepdims=True) * (1.0 / (2 * F)) + 1e-06
        white = stacked * (1.0 / jnp.sqrt(power))
        imag_at = jnp.where(window >= 32, window + 8, window + 48)
        for half in range(2):
            lanes = pl.ds(half * 128, 128)
            part = white[:, half * 128 : (half + 1) * 128]
            held_ref[pl.ds(half * F * ROWS + window, F, stride=ROWS), :] = part[:F]
            held_ref[pl.ds(half * F * ROWS + imag_at, F, stride=ROWS), :] = part[F:]
    carry_ref[...] = carry

    @pl.when(step == pl.num_programs(0) - 1)
    def _():
        @pl.loop(0, F)
        def _(place):
            for half in range(2):
                start = pl.multiple_of(half * F * ROWS + place * ROWS, 8)
                out_ref[place, :, half * 128 : (half + 1) * 128] = held_ref[pl.ds(start, ROWS), :].astype(
                    jnp.bfloat16
                )


def spectra(tail, table, records):
    channels, samples = records.shape
    steps = samples // WL // STEP_WINDOWS
    return pl.pallas_call(
        spectra_kernel,
        grid=(steps,),
        out_shape=jax.ShapeDtypeStruct((F, ROWS, channels), jnp.bfloat16),
        in_specs=[
            pl.BlockSpec(tail.shape, lambda i: (0, 0)),
            pl.BlockSpec(table.shape, lambda i: (0, 0)),
            pl.BlockSpec((channels, STEP_WINDOWS * WL), lambda i: (0, i)),
        ],
        out_specs=pl.BlockSpec((F, ROWS, channels), lambda i: (0, 0, 0)),
        scratch_shapes=[
            pltpu.VMEM((2 * F, channels), jnp.float32),
            pltpu.VMEM((2 * F * ROWS, 128), jnp.float32),
        ],
        compiler_params=pltpu.CompilerParams(vmem_limit_bytes=VMEM),
        name="spectra",
    )(tail, table, records)


def rotated(rows):
    layers = []
    for start in range(0, rows.shape[0], ROWS):
        first, second, mixed, fourth, fifth = (
            rows[start + TILE * t : start + TILE * (t + 1)] for t in range(5)
        )
        wide = mixed.astype(jnp.float32)
        turned = jnp.concatenate([wide[8:], -wide[:8]], axis=0).astype(jnp.bfloat16)
        layers += [fourth, fifth, turned, -first, -second]
    return jnp.concatenate(layers, axis=0)


TN = (((0,), (0,)), ((), ()))


def cross_kernel(scale, plan_ref, core_ref, own_ref, own_other_ref, mate_ref, mate_other_ref, out_ref):
    del plan_ref, core_ref
    own = jnp.concatenate([own_ref[0], own_other_ref[0]], axis=0)
    mate = jnp.concatenate([mate_ref[0], mate_other_ref[0]], axis=0)
    out_ref[0, 0] = (
        lax.dot_general(mate, own, TN, preferred_element_type=jnp.float32) * scale
    ).astype(jnp.bfloat16)
    out_ref[0, 1] = (
        lax.dot_general(mate, rotated(own), TN, preferred_element_type=jnp.float32) * scale
    ).astype(jnp.bfloat16)


def cross(plan, core, here, other, scale):
    blocks, depth, channels = here.shape
    own = pl.BlockSpec((1, depth, channels), lambda c, plan_ref, core_ref: (c, 0, 0))
    mate = pl.BlockSpec((1, depth, channels), lambda c, plan_ref, core_ref: (plan_ref[core_ref[0], c], 0, 0))
    return pl.pallas_call(
        functools.partial(cross_kernel, scale),
        grid_spec=pltpu.PrefetchScalarGridSpec(
            num_scalar_prefetch=2,
            grid=(blocks,),
            in_specs=[own, own, mate, mate],
            out_specs=pl.BlockSpec((1, 2, channels, channels), lambda c, plan_ref, core_ref: (c, 0, 0, 0)),
        ),
        out_shape=jax.ShapeDtypeStruct((blocks, 2, channels, channels), jnp.bfloat16),
        compiler_params=pltpu.CompilerParams(vmem_limit_bytes=VMEM),
        name="cross",
    )(plan, core, here, other, here, other)


def join_kernel(core_ref, mine_ref, other_ref, out_ref):
    core = core_ref[0]
    mine = mine_ref[0].astype(jnp.float32)
    other = other_ref[0].astype(jnp.float32)
    out_ref[0, core] = mine
    out_ref[0, 1 - core] = other


def join(core, mine, other):
    bins, halves, rows, channels = other.shape
    return pl.pallas_call(
        join_kernel,
        grid_spec=pltpu.PrefetchScalarGridSpec(
            num_scalar_prefetch=1,
            grid=(bins,),
            in_specs=[
                pl.BlockSpec((1, halves, rows, channels), lambda i, core_ref: (bins * core_ref[0] + i, 0, 0, 0)),
                pl.BlockSpec((1, halves, rows, channels), lambda i, core_ref: (i, 0, 0, 0)),
            ],
            out_specs=pl.BlockSpec((1, ROUNDS, halves, rows, channels), lambda i, core_ref: (i, 0, 0, 0, 0)),
        ),
        out_shape=jax.ShapeDtypeStruct((bins, ROUNDS, halves, rows, channels), jnp.float32),
        compiler_params=pltpu.CompilerParams(vmem_limit_bytes=VMEM),
        name="join",
    )(core, mine, other)


def on_device(dft, records, fir_taps, plan):
    channels, samples_here = records.shape
    chips = lax.axis_size("chip")
    cores = lax.axis_size("core")
    blocks = lax.axis_size("chan")
    core = lax.axis_index("core").astype(jnp.int32)
    count = chips * cores
    tail = lax.ppermute(
        records[:, samples_here - WL // 2 :], ("chip", "core"), [(i, i + 1) for i in range(count - 1)]
    )
    swap = [(0, 1), (1, 0)]
    scale = 1.0 / math.sqrt(samples_here // WL * count)
    white = spectra(tail, make_table(fir_taps, dft), records)
    here = lax.all_to_all(white, ("chan", "chip"), 0, 0, tiled=True)
    here = here.reshape(blocks, chips * ROWS, channels)
    other = lax.ppermute(here, "core", swap)
    core = core.reshape(1)
    products = cross(plan, core, here, other, scale)
    mine = lax.all_to_all(products, "chan", 0, 0, tiled=True)
    bins = blocks // cores
    away = lax.dynamic_slice_in_dim(mine, bins * (1 - core[0]), bins, 0)
    return join(core, mine, lax.ppermute(away, "core", swap))


def solution(mesh):
    blocks, count = mesh.devices.shape
    chips = count // 2
    inner = Mesh(mesh.devices.reshape(blocks, chips, 2), ("chan", "chip", "core"))
    dft = dft_rows(chips, blocks)

    def step(records, fir_taps, plan):
        return jax.shard_map(
            on_device,
            mesh=inner,
            in_specs=(P(), P("chan", ("chip", "core")), P(), P()),
            out_specs=P(("chip", "core"), None, None, None, "chan"),
            check_vma=False,
        )(jnp.asarray(dft), records, fir_taps, plan)

    return step
```

```python
import functools
import math

import jax
import jax.numpy as jnp
import numpy as np
from jax import lax
from jax.experimental import pallas as pl
from jax.experimental.pallas import tpu as pltpu
from jax.sharding import Mesh
from jax.sharding import PartitionSpec as P

WL = 256
F = 64
TAPS = 64
ROUNDS = 2
STEP_WINDOWS = 8
PIECES = 3
TILE = 16
VMEM = 50 * 1024 * 1024
SMALL_VMEM = 8 * 1024 * 1024
CALLS = ((2, 4, 6, 5), (3, 0, 7, 1))


def dft_rows(chips, blocks):
    place = np.arange(F)
    bin_number = blocks * (place % chips) + place // chips + 1
    phase = np.arange(WL)[None, :] * bin_number[:, None] % WL * (2.0 * math.pi / WL)
    return np.concatenate([np.cos(phase), -np.sin(phase)]).astype(np.float32)


def in_pieces(table):
    pieces = []
    rest = table
    for _ in range(PIECES):
        piece = rest.astype(jnp.bfloat16).astype(jnp.float32)
        pieces.append(piece)
        rest = rest - piece
    return pieces


def table_kernel(taps_ref, dft_ref, main_ref, before_ref, order_ref):
    lane = lax.broadcasted_iota(jnp.int32, (1, 2 * WL), 1)
    reversed_taps = jnp.zeros((1, 2 * WL), jnp.float32)
    for tap in range(TAPS):
        reversed_taps = jnp.where(lane == TAPS - 1 - tap, taps_ref[tap], reversed_taps)
    spread = jnp.broadcast_to(reversed_taps, (WL, 2 * WL))
    toeplitz = pltpu.roll(spread, WL - TAPS + 1, 1, stride=1, stride_axis=0)
    combined = jnp.dot(
        dft_ref[...], toeplitz, precision=lax.Precision.HIGHEST, preferred_element_type=jnp.float32
    )
    main_ref[...] = jnp.concatenate(in_pieces(combined[:, WL:]), axis=0).astype(jnp.bfloat16)
    high, middle, low = in_pieces(combined[:, WL // 2 : WL])
    left = lax.broadcasted_iota(jnp.int32, high.shape, 1) < TAPS
    first = jnp.where(left, pltpu.roll(high, TAPS, 1), middle)
    second = jnp.where(left, pltpu.roll(low, TAPS, 1), 0.0)
    before_ref[...] = jnp.concatenate([first, second], axis=1).astype(jnp.bfloat16)
    row = lax.broadcasted_iota(jnp.int32, order_ref.shape, 0)
    column = lax.broadcasted_iota(jnp.int32, order_ref.shape, 1)
    source = (row & 7) * 32 + ((row >> 3) & 1) * 16 + (row >> 4)
    order_ref[...] = jnp.where(column == source, 1.0, 0.0).astype(jnp.bfloat16)


IN_VMEM = pl.BlockSpec(memory_space=pltpu.VMEM)
IN_SMEM = pl.BlockSpec(memory_space=pltpu.SMEM)
IN_HBM = pl.BlockSpec(memory_space=pltpu.HBM)


def make_tables(fir_taps, dft):
    rows = (PIECES * 2 * F, 2 * F, WL)
    return pl.pallas_call(
        table_kernel,
        out_shape=[jax.ShapeDtypeStruct((count, WL), jnp.bfloat16) for count in rows],
        in_specs=[IN_SMEM, IN_VMEM],
        out_specs=[IN_VMEM] * 3,
        compiler_params=pltpu.CompilerParams(vmem_limit_bytes=SMALL_VMEM),
        name="table",
    )(fir_taps, dft)


NT = (((1,), (1,)), ((), ()))


def last_samples(samples):
    end = samples[:, samples.shape[1] - TAPS :]
    return jnp.concatenate([end] * (WL // TAPS), axis=1)


def spectra_kernel(
    tail_ref, main_ref, before_ref, order_ref, records_ref, out_ref, samples_ref, carry_ref, held_ref, sems
):
    groups = samples_ref.shape[0]
    width = STEP_WINDOWS * WL
    count = 2 * F

    def fetch(group):
        source = records_ref.at[:, pl.ds(pl.multiple_of(group * width, width), width)]
        return pltpu.make_async_copy(source, samples_ref.at[group], sems.at[group])

    for group in range(groups):
        fetch(group).start()
    before = before_ref[...]
    carry_ref[...] = lax.dot_general(
        before, last_samples(tail_ref[...]), NT, preferred_element_type=jnp.float32
    )

    @pl.loop(0, groups)
    def _(group):
        fetch(group).wait()
        carry = carry_ref[...]
        for inner in range(STEP_WINDOWS):
            samples = samples_ref[group, :, inner * WL : (inner + 1) * WL]
            rows = lax.dot_general(main_ref[...], samples, NT, preferred_element_type=jnp.float32)
            stacked = rows[2 * count :] + rows[count : 2 * count] + carry + rows[:count]
            carry = lax.dot_general(
                before, last_samples(samples), NT, preferred_element_type=jnp.float32
            )
            power = jnp.sum(stacked * stacked, axis=0, keepdims=True) * (1.0 / count) + 1e-06
            held_ref[inner] = (stacked * (1.0 / jnp.sqrt(power))).astype(jnp.bfloat16)
        carry_ref[...] = carry
        for part in range(F // TILE):
            rows = []
            for inner in range(STEP_WINDOWS):
                for start in (part * TILE, F + part * TILE):
                    rows.append(held_ref[inner, start : start + TILE, :])
            placed = jnp.dot(
                order_ref[...], jnp.concatenate(rows, axis=0), preferred_element_type=jnp.float32
            ).astype(jnp.bfloat16)
            at = pl.ds(pl.multiple_of(group * TILE, TILE), TILE)
            for n in range(TILE):
                out_ref[part * TILE + n, at, :] = placed[n * TILE : (n + 1) * TILE]


def spectra(tail, tables, records):
    channels, samples = records.shape
    groups = samples // WL // STEP_WINDOWS
    return pl.pallas_call(
        spectra_kernel,
        out_shape=jax.ShapeDtypeStruct((F, groups * TILE, channels), jnp.bfloat16),
        in_specs=[IN_VMEM] * 4 + [IN_HBM],
        out_specs=IN_VMEM,
        scratch_shapes=[
            pltpu.VMEM((groups, channels, STEP_WINDOWS * WL), jnp.bfloat16),
            pltpu.VMEM((2 * F, channels), jnp.float32),
            pltpu.VMEM((STEP_WINDOWS, 2 * F, channels), jnp.bfloat16),
            pltpu.SemaphoreType.DMA((groups,)),
        ],
        compiler_params=pltpu.CompilerParams(vmem_limit_bytes=VMEM),
        name="spectra",
    )(tail, *tables, records)


def rotated(rows):
    wide = rows.astype(jnp.float32)
    layers = []
    for start in range(0, rows.shape[0], TILE):
        middle = start + TILE // 2
        layers += [wide[middle : start + TILE], -wide[start:middle]]
    return jnp.concatenate(layers, axis=0).astype(jnp.bfloat16)


TN = (((0,), (0,)), ((), ()))


def target(step, half, place, core):
    return place ^ (step // 2) ^ (half * ((step % 2) ^ core))


def cross_kernel(scale, steps, plan_ref, place_ref, here_ref, other_ref, *out_refs):
    half_blocks = here_ref.shape[0] // 2
    for step, out_ref in zip(steps, out_refs):
        own_at = target(step, half_blocks, place_ref[0], place_ref[1])
        mate_at = plan_ref[place_ref[1], own_at]
        own = jnp.concatenate([here_ref[own_at], other_ref[own_at]], axis=0)
        mate = jnp.concatenate([here_ref[mate_at], other_ref[mate_at]], axis=0)
        for half, rows in enumerate((own, rotated(own))):
            product = lax.dot_general(mate, rows, TN, preferred_element_type=jnp.float32) * scale
            out_ref[half] = product.astype(jnp.bfloat16)


def cross(steps, plan, place, here, other, scale):
    depth, channels = here.shape[1:]
    return pl.pallas_call(
        functools.partial(cross_kernel, scale, steps),
        in_specs=[IN_SMEM, IN_SMEM, IN_VMEM, IN_VMEM],
        out_specs=[IN_VMEM] * len(steps),
        out_shape=[jax.ShapeDtypeStruct((2, channels, channels), jnp.bfloat16)] * len(steps),
        compiler_params=pltpu.CompilerParams(vmem_limit_bytes=SMALL_VMEM),
        cost_estimate=pl.CostEstimate(
            flops=len(steps) * 2 * 2 * 2 * depth * channels * channels,
            bytes_accessed=len(steps) * (8 * depth * channels + 4 * channels * channels),
            transcendentals=0,
        ),
        name="cross",
    )(plan, place, here, other)


def join_kernel(steps, bins, place_ref, *refs):
    parts, (out_ref, wide_ref, sems) = refs[:-3], refs[-3:]
    copies = []
    for n, step in enumerate(steps):
        own_bin = (place_ref[0] % bins) ^ (step // 2)
        round_index = (place_ref[0] // bins) ^ place_ref[1] ^ (step % 2)
        wide_ref[n] = parts[n][...].astype(jnp.float32)
        copy = pltpu.make_async_copy(wide_ref.at[n], out_ref.at[own_bin, round_index], sems.at[n])
        copy.start()
        copies.append(copy)
    for copy in copies:
        copy.wait()


def join(steps, place, parts, bins):
    halves, rows, channels = parts[0].shape
    return pl.pallas_call(
        functools.partial(join_kernel, steps, bins),
        in_specs=[IN_SMEM] + [IN_VMEM] * len(steps),
        out_specs=pl.BlockSpec(memory_space=pl.ANY),
        out_shape=jax.ShapeDtypeStruct((bins, ROUNDS, halves, rows, channels), jnp.float32),
        scratch_shapes=[
            pltpu.VMEM((len(steps), halves, rows, channels), jnp.float32),
            pltpu.SemaphoreType.DMA((len(steps),)),
        ],
        compiler_params=pltpu.CompilerParams(vmem_limit_bytes=SMALL_VMEM),
        name="join",
    )(place, *parts)


def on_device(dft, records, fir_taps, plan):
    channels, samples_here = records.shape
    chips = lax.axis_size("chip")
    cores = lax.axis_size("core")
    blocks = lax.axis_size("chan")
    core = lax.axis_index("core").astype(jnp.int32)
    count = chips * cores
    tail = lax.ppermute(
        records[:, samples_here - WL // 2 :], ("chip", "core"), [(i, i + 1) for i in range(count - 1)]
    )
    swap = [(0, 1), (1, 0)]
    scale = 1.0 / math.sqrt(samples_here // WL * count)
    white = spectra(tail, make_tables(fir_taps, dft), records)
    here = lax.all_to_all(white, ("chan", "chip"), 0, 0, tiled=True)
    here = here.reshape(blocks, chips * white.shape[1], channels)
    other = lax.ppermute(here, "core", swap)
    half = blocks // 2
    place = jnp.stack([lax.axis_index("chan").astype(jnp.int32), core])
    steps = [step for call in CALLS for step in call]
    parts = []
    for call in CALLS:
        products = cross(call, plan, place, here, other, scale)
        here, other, *products = lax.optimization_barrier((here, other, *products))
        for step, product in zip(call, products):
            route = [
                (j * cores + h, target(step, half, j, h) * cores + j // half)
                for j in range(blocks)
                for h in range(cores)
            ]
            parts.append(lax.ppermute(product, ("chan", "core"), route))
    return join(steps, place, parts, half)


def solution(mesh):
    blocks, count = mesh.devices.shape
    chips = count // 2
    inner = Mesh(mesh.devices.reshape(blocks, chips, 2), ("chan", "chip", "core"))
    dft = dft_rows(chips, blocks)

    def step(records, fir_taps, plan):
        return jax.shard_map(
            on_device,
            mesh=inner,
            in_specs=(P(), P("chan", ("chip", "core")), P(), P()),
            out_specs=P(("chip", "core"), None, None, None, "chan"),
            check_vma=False,
        )(jnp.asarray(dft), records, fir_taps, plan)

    return step
```

```python
import functools
import math

import jax
import jax.numpy as jnp
import numpy as np
from jax import lax
from jax.experimental import pallas as pl
from jax.experimental.pallas import tpu as pltpu
from jax.sharding import Mesh
from jax.sharding import PartitionSpec as P

WL = 256
F = 64
TAPS = 64
ROUNDS = 2
STEP_WINDOWS = 8
FIRST_PARTS = 4
PIECES = 3
TILE = 16
VMEM = 32 * 1024 * 1024
SMALL_VMEM = 8 * 1024 * 1024
FIRST = 2
CALLS = ((6, 4, 3), (7, 5, 0, 1))
JOINED_EARLY = 5


def dft_rows(chips, blocks):
    place = np.arange(F)
    bin_number = blocks * (place % chips) + place // chips + 1
    phase = np.arange(WL)[None, :] * bin_number[:, None] % WL * (2.0 * math.pi / WL)
    return np.concatenate([np.cos(phase), -np.sin(phase)]).astype(np.float32)


def in_pieces(table):
    pieces = []
    rest = table
    for _ in range(PIECES):
        piece = rest.astype(jnp.bfloat16).astype(jnp.float32)
        pieces.append(piece)
        rest = rest - piece
    return pieces


def table_kernel(taps_at, dft_at, main_ref, before_ref, order_ref, taps_ref, dft_ref, sems):
    taps_copy = pltpu.make_async_copy(taps_at, taps_ref, sems.at[0])
    dft_copy = pltpu.make_async_copy(dft_at, dft_ref, sems.at[1])
    taps_copy.start()
    dft_copy.start()
    row = lax.broadcasted_iota(jnp.int32, order_ref.shape, 0)
    column = lax.broadcasted_iota(jnp.int32, order_ref.shape, 1)
    source = (row & 7) * 32 + ((row >> 3) & 1) * 16 + (row >> 4)
    order_ref[...] = jnp.where(column == source, 1.0, 0.0).astype(jnp.bfloat16)
    taps_copy.wait()
    lane = lax.broadcasted_iota(jnp.int32, (1, 2 * WL), 1)
    reversed_taps = jnp.zeros((1, 2 * WL), jnp.float32)
    for tap in range(TAPS):
        reversed_taps = jnp.where(lane == TAPS - 1 - tap, taps_ref[tap], reversed_taps)
    spread = jnp.broadcast_to(reversed_taps, (WL, 2 * WL))
    toeplitz = pltpu.roll(spread, WL - TAPS + 1, 1, stride=1, stride_axis=0)
    dft_copy.wait()
    combined = jnp.dot(
        dft_ref[...], toeplitz, precision=lax.Precision.HIGHEST, preferred_element_type=jnp.float32
    )
    main_ref[...] = jnp.concatenate(in_pieces(combined[:, WL:]), axis=0).astype(jnp.bfloat16)
    high, middle, low = in_pieces(combined[:, WL // 2 : WL])
    left = lax.broadcasted_iota(jnp.int32, high.shape, 1) < TAPS
    first = jnp.where(left, pltpu.roll(high, TAPS, 1), middle)
    second = jnp.where(left, pltpu.roll(low, TAPS, 1), 0.0)
    before_ref[...] = jnp.concatenate([first, second], axis=1).astype(jnp.bfloat16)


IN_VMEM = pl.BlockSpec(memory_space=pltpu.VMEM)
IN_SMEM = pl.BlockSpec(memory_space=pltpu.SMEM)
IN_HBM = pl.BlockSpec(memory_space=pltpu.HBM)


def make_tables(fir_taps, dft):
    rows = (PIECES * 2 * F, 2 * F, WL)
    return pl.pallas_call(
        table_kernel,
        out_shape=[jax.ShapeDtypeStruct((count, WL), jnp.bfloat16) for count in rows],
        in_specs=[IN_HBM, IN_HBM],
        out_specs=[IN_VMEM] * 3,
        scratch_shapes=[
            pltpu.SMEM(fir_taps.shape, jnp.float32),
            pltpu.VMEM(dft.shape, jnp.float32),
            pltpu.SemaphoreType.DMA((2,)),
        ],
        compiler_params=pltpu.CompilerParams(vmem_limit_bytes=SMALL_VMEM),
        name="table",
    )(*(pltpu.with_memory_space_constraint(given, pltpu.HBM) for given in (fir_taps, dft)))


NT = (((1,), (1,)), ((), ()))


def last_samples(samples):
    end = samples[:, samples.shape[1] - TAPS :]
    return jnp.concatenate([end] * (WL // TAPS), axis=1)


def spectra_kernel(
    tail_ref,
    main_ref,
    before_ref,
    order_ref,
    records_ref,
    out_ref,
    samples_ref,
    carry_ref,
    held_ref,
    white_ref,
    in_sems,
    out_sems,
):
    groups = samples_ref.shape[0]
    width = STEP_WINDOWS * WL
    first = width // FIRST_PARTS
    count = 2 * F
    before = before_ref[...]

    def fetch_first(part):
        lanes = pl.ds(part * first, first)
        return pltpu.make_async_copy(
            records_ref.at[:, lanes], samples_ref.at[0, :, lanes], in_sems.at[groups + part]
        )

    def fetch(group):
        source = records_ref.at[:, pl.ds(pl.multiple_of(group * width, width), width)]
        return pltpu.make_async_copy(source, samples_ref.at[group], in_sems.at[group])

    def rows_of(group):
        return pl.ds(pl.multiple_of(group * TILE, TILE), TILE)

    def send(group):
        at = rows_of(group)
        return pltpu.make_async_copy(white_ref.at[:, at, :], out_ref.at[:, at, :], out_sems.at[group])

    def make(group):
        carry = carry_ref[...]
        for inner in range(STEP_WINDOWS):
            if isinstance(group, int) and inner * WL % first == 0:
                fetch_first(inner * WL // first).wait()
            samples = samples_ref[group, :, inner * WL : (inner + 1) * WL]
            rows = lax.dot_general(main_ref[...], samples, NT, preferred_element_type=jnp.float32)
            stacked = rows[2 * count :] + rows[count : 2 * count] + carry + rows[:count]
            carry = lax.dot_general(
                before, last_samples(samples), NT, preferred_element_type=jnp.float32
            )
            power = jnp.sum(stacked * stacked, axis=0, keepdims=True) * (1.0 / count) + 1e-06
            held_ref[inner] = (stacked * (1.0 / jnp.sqrt(power))).astype(jnp.bfloat16)
        carry_ref[...] = carry

    def place(group):
        for part in range(F // TILE):
            rows = []
            for inner in range(STEP_WINDOWS):
                for start in (part * TILE, F + part * TILE):
                    rows.append(held_ref[inner, start : start + TILE, :])
            placed = jnp.dot(
                order_ref[...], jnp.concatenate(rows, axis=0), preferred_element_type=jnp.float32
            ).astype(jnp.bfloat16)
            for n in range(TILE):
                white_ref[part * TILE + n, rows_of(group), :] = placed[n * TILE : (n + 1) * TILE]

    for part in range(FIRST_PARTS):
        fetch_first(part).start()
    for group in range(1, groups):
        fetch(group).start()
    carry_ref[...] = lax.dot_general(
        before, last_samples(tail_ref[...]), NT, preferred_element_type=jnp.float32
    )
    make(0)

    @pl.loop(1, groups)
    def _(group):
        fetch(group).wait()
        place(group - 1)
        make(group)
        send(group - 1).start()

    place(groups - 1)
    send(groups - 1).start()
    for group in range(groups):
        send(group).wait()


def spectra(tail, tables, records):
    channels, samples = records.shape
    groups = samples // WL // STEP_WINDOWS
    result = (F, groups * TILE, channels)
    return pl.pallas_call(
        spectra_kernel,
        out_shape=pltpu.HBM(result, jnp.bfloat16),
        in_specs=[IN_VMEM] * 4 + [IN_HBM],
        out_specs=IN_HBM,
        scratch_shapes=[
            pltpu.VMEM((groups, channels, STEP_WINDOWS * WL), jnp.bfloat16),
            pltpu.VMEM((2 * F, channels), jnp.float32),
            pltpu.VMEM((STEP_WINDOWS, 2 * F, channels), jnp.bfloat16),
            pltpu.VMEM(result, jnp.bfloat16),
            pltpu.SemaphoreType.DMA((groups + FIRST_PARTS,)),
            pltpu.SemaphoreType.DMA((groups,)),
        ],
        compiler_params=pltpu.CompilerParams(vmem_limit_bytes=VMEM),
        name="spectra",
    )(tail, *tables, pltpu.with_memory_space_constraint(records, pltpu.HBM))


def rotated(rows):
    wide = rows.astype(jnp.float32)
    layers = []
    for start in range(0, rows.shape[0], TILE):
        middle = start + TILE // 2
        layers += [wide[middle : start + TILE], -wide[start:middle]]
    return jnp.concatenate(layers, axis=0).astype(jnp.bfloat16)


TN = (((0,), (0,)), ((), ()))


def target(step, half, place, core):
    return place ^ (step // 2) ^ (half * ((step % 2) ^ core))


def cross_kernel(scale, steps, plan_ref, place_ref, here_ref, other_ref, *refs):
    half_blocks = here_ref.shape[0] // 2
    picked = other_ref.shape[0] == 2
    out_refs = refs[-len(steps) :]
    for step, out_ref in zip(steps, out_refs):
        own_at = target(step, half_blocks, place_ref[0], place_ref[1])
        mate_at = plan_ref[place_ref[1], own_at]
        own = jnp.concatenate([here_ref[own_at], other_ref[0 if picked else own_at]], axis=0)
        mate = jnp.concatenate([here_ref[mate_at], other_ref[1 if picked else mate_at]], axis=0)
        for half, rows in enumerate((own, rotated(own))):
            product = lax.dot_general(mate, rows, TN, preferred_element_type=jnp.float32) * scale
            out_ref[half] = product.astype(jnp.bfloat16)


def cross(steps, plan, place, here, other, scale):
    depth, channels = here.shape[1:]
    return pl.pallas_call(
        functools.partial(cross_kernel, scale, steps),
        in_specs=[IN_SMEM, IN_SMEM, IN_VMEM, IN_VMEM],
        out_specs=[IN_VMEM] * len(steps),
        out_shape=[jax.ShapeDtypeStruct((2, channels, channels), jnp.bfloat16)] * len(steps),
        compiler_params=pltpu.CompilerParams(vmem_limit_bytes=SMALL_VMEM),
        cost_estimate=pl.CostEstimate(
            flops=len(steps) * 2 * 2 * 2 * depth * channels * channels,
            bytes_accessed=len(steps) * (8 * depth * channels + 4 * channels * channels),
            transcendentals=0,
        ),
        name="cross",
    )(plan, place, here, other)


def join_kernel(steps, bins, place_ref, *refs):
    parts, (out_ref, wide_ref, sems) = refs[: len(steps)], refs[-3:]
    copies = []
    for n, step in enumerate(steps):
        own_bin = (place_ref[0] % bins) ^ (step // 2)
        round_index = (place_ref[0] // bins) ^ place_ref[1] ^ (step % 2)
        wide_ref[n] = parts[n][...].astype(jnp.float32)
        copy = pltpu.make_async_copy(wide_ref.at[n], out_ref.at[own_bin, round_index], sems.at[n])
        copy.start()
        copies.append(copy)
    for copy in copies:
        copy.wait()


def join(steps, place, parts, bins, earlier=()):
    halves, rows, channels = parts[0].shape
    return pl.pallas_call(
        functools.partial(join_kernel, steps, bins),
        in_specs=[IN_SMEM] + [IN_VMEM] * len(steps) + [IN_HBM] * len(earlier),
        out_specs=IN_HBM,
        out_shape=jax.ShapeDtypeStruct((bins, ROUNDS, halves, rows, channels), jnp.float32),
        scratch_shapes=[
            pltpu.VMEM((len(steps), halves, rows, channels), jnp.float32),
            pltpu.SemaphoreType.DMA((len(steps),)),
        ],
        input_output_aliases={1 + len(steps): 0} if earlier else {},
        compiler_params=pltpu.CompilerParams(vmem_limit_bytes=SMALL_VMEM),
        cost_estimate=pl.CostEstimate(
            flops=0, bytes_accessed=len(steps) * 6 * halves * rows * channels, transcendentals=0
        ),
        name="join",
    )(place, *parts, *earlier)


def on_device(dft, records, fir_taps, plan):
    channels, samples_here = records.shape
    chips = lax.axis_size("chip")
    cores = lax.axis_size("core")
    blocks = lax.axis_size("chan")
    core = lax.axis_index("core").astype(jnp.int32)
    count = chips * cores
    tail = lax.ppermute(
        records[:, samples_here - WL // 2 :], ("chip", "core"), [(i, i + 1) for i in range(count - 1)]
    )
    swap = [(0, 1), (1, 0)]
    scale = 1.0 / math.sqrt(samples_here // WL * count)
    white = spectra(tail, make_tables(fir_taps, dft), records)
    here = lax.all_to_all(white, ("chan", "chip"), 0, 0, tiled=True)
    here = here.reshape(blocks, chips * white.shape[1], channels)
    half = blocks // 2
    place = jnp.stack([lax.axis_index("chan").astype(jnp.int32), core])
    away_at = target(FIRST, half, place[0], 1 - core)
    away = [here[away_at], here[plan[1 - core, away_at]]]
    first_other = lax.ppermute(jnp.stack(away), "core", swap)
    here, first_other = lax.optimization_barrier((here, first_other))
    other = lax.ppermute(here, "core", swap)
    parts = []
    last = ()
    for call in ((FIRST,), *CALLS):
        products = cross(call, plan, place, here, first_other if call == (FIRST,) else other, scale)
        if call == (FIRST,):
            here, *products = lax.optimization_barrier((here, *products))
        else:
            here, other, *products = lax.optimization_barrier((here, other, *products))
        for step, product in zip(call, products):
            route = [
                (j * cores + h, target(step, half, j, h) * cores + j // half)
                for j in range(blocks)
                for h in range(cores)
            ]
            parts.append(lax.ppermute(product, ("chan", "core"), route))
    steps = [FIRST] + [step for call in CALLS for step in call]
    if JOINED_EARLY:
        last = [join(steps[:JOINED_EARLY], place, parts[:JOINED_EARLY], half)]
    return join(steps[JOINED_EARLY:], place, parts[JOINED_EARLY:], half, last)


def solution(mesh):
    blocks, count = mesh.devices.shape
    chips = count // 2
    inner = Mesh(mesh.devices.reshape(blocks, chips, 2), ("chan", "chip", "core"))
    dft = dft_rows(chips, blocks)

    def step(records, fir_taps, plan):
        return jax.shard_map(
            on_device,
            mesh=inner,
            in_specs=(P(), P("chan", ("chip", "core")), P(), P()),
            out_specs=P(("chip", "core"), None, None, None, "chan"),
            check_vma=False,
        )(jnp.asarray(dft), records, fir_taps, plan)

    return step
```

```python
import functools
import math

import jax
import jax.numpy as jnp
import numpy as np
from jax import lax
from jax.experimental import pallas as pl
from jax.experimental.pallas import tpu as pltpu
from jax.sharding import Mesh
from jax.sharding import PartitionSpec as P

WL = 256
F = 64
TAPS = 64
ROUNDS = 2
STEP_WINDOWS = 8
FIRST_PARTS = 1
PIECES = 3
TILE = 16
VMEM = 32 * 1024 * 1024
SMALL_VMEM = 8 * 1024 * 1024
FIRST = 2
CALLS = ((6, 4, 3), (7, 5), (0, 1))
JOINED_LAST = (5, 0, 1)


def dft_rows(chips, blocks):
    place = np.arange(F)
    bin_number = blocks * (place % chips) + place // chips + 1
    phase = np.arange(WL)[None, :] * bin_number[:, None] % WL * (2.0 * math.pi / WL)
    return np.concatenate([np.cos(phase), -np.sin(phase)]).astype(np.float32)


def in_pieces(table):
    pieces = []
    rest = table
    for _ in range(PIECES):
        piece = rest.astype(jnp.bfloat16).astype(jnp.float32)
        pieces.append(piece)
        rest = rest - piece
    return pieces


def table_kernel(taps_at, dft_at, main_ref, before_ref, order_ref, taps_ref, dft_ref, sems):
    taps_copy = pltpu.make_async_copy(taps_at, taps_ref, sems.at[0])
    dft_copy = pltpu.make_async_copy(dft_at, dft_ref, sems.at[1])
    taps_copy.start()
    dft_copy.start()
    row = lax.broadcasted_iota(jnp.int32, order_ref.shape, 0)
    column = lax.broadcasted_iota(jnp.int32, order_ref.shape, 1)
    source = (row & 7) * 32 + ((row >> 3) & 1) * 16 + (row >> 4)
    order_ref[...] = jnp.where(column == source, 1.0, 0.0).astype(jnp.bfloat16)
    taps_copy.wait()
    lane = lax.broadcasted_iota(jnp.int32, (1, 2 * WL), 1)
    reversed_taps = jnp.zeros((1, 2 * WL), jnp.float32)
    for tap in range(TAPS):
        reversed_taps = jnp.where(lane == TAPS - 1 - tap, taps_ref[tap], reversed_taps)
    spread = jnp.broadcast_to(reversed_taps, (WL, 2 * WL))
    toeplitz = pltpu.roll(spread, WL - TAPS + 1, 1, stride=1, stride_axis=0)
    dft_copy.wait()
    combined = jnp.dot(
        dft_ref[...], toeplitz, precision=lax.Precision.HIGHEST, preferred_element_type=jnp.float32
    )
    main_ref[...] = jnp.concatenate(in_pieces(combined[:, WL:]), axis=0).astype(jnp.bfloat16)
    high, middle, low = in_pieces(combined[:, WL // 2 : WL])
    left = lax.broadcasted_iota(jnp.int32, high.shape, 1) < TAPS
    first = jnp.where(left, pltpu.roll(high, TAPS, 1), middle)
    second = jnp.where(left, pltpu.roll(low, TAPS, 1), 0.0)
    before_ref[...] = jnp.concatenate([first, second], axis=1).astype(jnp.bfloat16)


IN_VMEM = pl.BlockSpec(memory_space=pltpu.VMEM)
IN_SMEM = pl.BlockSpec(memory_space=pltpu.SMEM)
IN_HBM = pl.BlockSpec(memory_space=pltpu.HBM)


def make_tables(fir_taps, dft):
    rows = (PIECES * 2 * F, 2 * F, WL)
    return pl.pallas_call(
        table_kernel,
        out_shape=[jax.ShapeDtypeStruct((count, WL), jnp.bfloat16) for count in rows],
        in_specs=[IN_HBM, IN_HBM],
        out_specs=[IN_VMEM] * 3,
        scratch_shapes=[
            pltpu.SMEM(fir_taps.shape, jnp.float32),
            pltpu.VMEM(dft.shape, jnp.float32),
            pltpu.SemaphoreType.DMA((2,)),
        ],
        compiler_params=pltpu.CompilerParams(vmem_limit_bytes=SMALL_VMEM),
        name="table",
    )(*(pltpu.with_memory_space_constraint(given, pltpu.HBM) for given in (fir_taps, dft)))


def last_samples(across):
    return jnp.concatenate([across[across.shape[0] - TAPS :]] * (WL // TAPS), axis=0)


def spectra_kernel(
    tail_ref,
    main_ref,
    before_ref,
    order_ref,
    records_ref,
    out_ref,
    samples_ref,
    carry_ref,
    held_ref,
    white_ref,
    in_sems,
    out_sems,
):
    groups = samples_ref.shape[0]
    width = STEP_WINDOWS * WL
    first = width // FIRST_PARTS
    count = 2 * F
    before = before_ref[...]

    def fetch_first(part):
        lanes = pl.ds(part * first, first)
        return pltpu.make_async_copy(
            records_ref.at[:, lanes], samples_ref.at[0, :, lanes], in_sems.at[groups + part]
        )

    def fetch(group):
        source = records_ref.at[:, pl.ds(pl.multiple_of(group * width, width), width)]
        return pltpu.make_async_copy(source, samples_ref.at[group], in_sems.at[group])

    def rows_of(group):
        return pl.ds(pl.multiple_of(group * TILE, TILE), TILE)

    def send(group):
        at = rows_of(group)
        return pltpu.make_async_copy(white_ref.at[:, at, :], out_ref.at[:, at, :], out_sems.at[group])

    def make(group):
        carry = carry_ref[...]
        for inner in range(STEP_WINDOWS):
            if isinstance(group, int) and inner * WL % first == 0:
                fetch_first(inner * WL // first).wait()
            across = samples_ref[group, :, inner * WL : (inner + 1) * WL].T
            rows = jnp.dot(main_ref[...], across, preferred_element_type=jnp.float32)
            stacked = rows[2 * count :] + rows[count : 2 * count] + carry + rows[:count]
            carry = jnp.dot(before, last_samples(across), preferred_element_type=jnp.float32)
            power = jnp.sum(stacked * stacked, axis=0, keepdims=True) * (1.0 / count) + 1e-06
            held_ref[inner] = (stacked * (1.0 / jnp.sqrt(power))).astype(jnp.bfloat16)
        carry_ref[...] = carry

    def place(group):
        for part in range(F // TILE):
            rows = []
            for inner in range(STEP_WINDOWS):
                for start in (part * TILE, F + part * TILE):
                    rows.append(held_ref[inner, start : start + TILE, :])
            placed = jnp.dot(
                order_ref[...], jnp.concatenate(rows, axis=0), preferred_element_type=jnp.float32
            ).astype(jnp.bfloat16)
            for n in range(TILE):
                white_ref[part * TILE + n, rows_of(group), :] = placed[n * TILE : (n + 1) * TILE]

    for part in range(FIRST_PARTS):
        fetch_first(part).start()
    for group in range(1, groups):
        fetch(group).start()
    carry_ref[...] = jnp.dot(before, last_samples(tail_ref[...].T), preferred_element_type=jnp.float32)
    make(0)

    @pl.loop(1, groups)
    def _(group):
        fetch(group).wait()
        place(group - 1)
        make(group)
        send(group - 1).start()

    place(groups - 1)
    send(groups - 1).start()
    for group in range(groups):
        send(group).wait()


def spectra(tail, tables, records):
    channels, samples = records.shape
    groups = samples // WL // STEP_WINDOWS
    result = (F, groups * TILE, channels)
    return pl.pallas_call(
        spectra_kernel,
        out_shape=pltpu.HBM(result, jnp.bfloat16),
        in_specs=[IN_VMEM] * 4 + [IN_HBM],
        out_specs=IN_HBM,
        scratch_shapes=[
            pltpu.VMEM((groups, channels, STEP_WINDOWS * WL), jnp.bfloat16),
            pltpu.VMEM((2 * F, channels), jnp.float32),
            pltpu.VMEM((STEP_WINDOWS, 2 * F, channels), jnp.bfloat16),
            pltpu.VMEM(result, jnp.bfloat16),
            pltpu.SemaphoreType.DMA((groups + FIRST_PARTS,)),
            pltpu.SemaphoreType.DMA((groups,)),
        ],
        compiler_params=pltpu.CompilerParams(vmem_limit_bytes=VMEM),
        name="spectra",
    )(tail, *tables, pltpu.with_memory_space_constraint(records, pltpu.HBM))


def rotated(rows):
    wide = rows.astype(jnp.float32)
    layers = []
    for start in range(0, rows.shape[0], TILE):
        middle = start + TILE // 2
        layers += [wide[middle : start + TILE], -wide[start:middle]]
    return jnp.concatenate(layers, axis=0).astype(jnp.bfloat16)


TN = (((0,), (0,)), ((), ()))


def target(step, half, place, core):
    return place ^ (step // 2) ^ (half * ((step % 2) ^ core))


def cross_kernel(scale, steps, plan_ref, place_ref, here_ref, other_ref, *refs):
    half_blocks = here_ref.shape[0] // 2
    picked = other_ref.shape[0] == 2
    out_refs = refs[-len(steps) :]
    for step, out_ref in zip(steps, out_refs):
        own_at = target(step, half_blocks, place_ref[0], place_ref[1])
        mate_at = plan_ref[place_ref[1], own_at]
        own = jnp.concatenate([here_ref[own_at], other_ref[0 if picked else own_at]], axis=0)
        mate = jnp.concatenate([here_ref[mate_at], other_ref[1 if picked else mate_at]], axis=0)
        for half, rows in enumerate((own, rotated(own))):
            product = lax.dot_general(mate, rows, TN, preferred_element_type=jnp.float32) * scale
            out_ref[half] = product.astype(jnp.bfloat16)


def cross(steps, plan, place, here, other, scale):
    depth, channels = here.shape[1:]
    return pl.pallas_call(
        functools.partial(cross_kernel, scale, steps),
        in_specs=[IN_SMEM, IN_SMEM, IN_VMEM, IN_VMEM],
        out_specs=[IN_VMEM] * len(steps),
        out_shape=[jax.ShapeDtypeStruct((2, channels, channels), jnp.bfloat16)] * len(steps),
        compiler_params=pltpu.CompilerParams(vmem_limit_bytes=SMALL_VMEM),
        cost_estimate=pl.CostEstimate(
            flops=len(steps) * 2 * 2 * 2 * depth * channels * channels,
            bytes_accessed=len(steps) * (8 * depth * channels + 4 * channels * channels),
            transcendentals=0,
        ),
        name="cross",
    )(plan, place, here, other)


def join_kernel(steps, bins, place_ref, *refs):
    parts, (out_ref, wide_ref, sems) = refs[: len(steps)], refs[-3:]
    copies = []
    for n, step in enumerate(steps):
        own_bin = (place_ref[0] % bins) ^ (step // 2)
        round_index = (place_ref[0] // bins) ^ place_ref[1] ^ (step % 2)
        wide_ref[n] = parts[n][...].astype(jnp.float32)
        copy = pltpu.make_async_copy(wide_ref.at[n], out_ref.at[own_bin, round_index], sems.at[n])
        copy.start()
        copies.append(copy)
    for copy in copies:
        copy.wait()


def join(steps, place, parts, bins, earlier=()):
    halves, rows, channels = parts[0].shape
    return pl.pallas_call(
        functools.partial(join_kernel, steps, bins),
        in_specs=[IN_SMEM] + [IN_VMEM] * len(steps) + [IN_HBM] * len(earlier),
        out_specs=IN_HBM,
        out_shape=jax.ShapeDtypeStruct((bins, ROUNDS, halves, rows, channels), jnp.float32),
        scratch_shapes=[
            pltpu.VMEM((len(steps), halves, rows, channels), jnp.float32),
            pltpu.SemaphoreType.DMA((len(steps),)),
        ],
        input_output_aliases={1 + len(steps): 0} if earlier else {},
        compiler_params=pltpu.CompilerParams(vmem_limit_bytes=SMALL_VMEM),
        cost_estimate=pl.CostEstimate(
            flops=0, bytes_accessed=len(steps) * 6 * halves * rows * channels, transcendentals=0
        ),
        name="join",
    )(place, *parts, *earlier)


def on_device(dft, records, fir_taps, plan):
    channels, samples_here = records.shape
    chips = lax.axis_size("chip")
    cores = lax.axis_size("core")
    blocks = lax.axis_size("chan")
    core = lax.axis_index("core").astype(jnp.int32)
    count = chips * cores
    tail = lax.ppermute(
        records[:, samples_here - WL // 2 :], ("chip", "core"), [(i, i + 1) for i in range(count - 1)]
    )
    swap = [(0, 1), (1, 0)]
    scale = 1.0 / math.sqrt(samples_here // WL * count)
    white = spectra(tail, make_tables(fir_taps, dft), records)
    here = lax.all_to_all(white, ("chan", "chip"), 0, 0, tiled=True)
    here = here.reshape(blocks, chips * white.shape[1], channels)
    half = blocks // 2
    place = jnp.stack([lax.axis_index("chan").astype(jnp.int32), core])
    away_at = target(FIRST, half, place[0], 1 - core)
    away = [here[away_at], here[plan[1 - core, away_at]]]
    first_other = lax.ppermute(jnp.stack(away), "core", swap)
    here, first_other = lax.optimization_barrier((here, first_other))
    other = lax.ppermute(here, "core", swap)
    parts = []
    for call in ((FIRST,), *CALLS):
        products = cross(call, plan, place, here, first_other if call == (FIRST,) else other, scale)
        if call == (FIRST,):
            here, *products = lax.optimization_barrier((here, *products))
        else:
            here, other, *products = lax.optimization_barrier((here, other, *products))
        for step, product in zip(call, products):
            route = [
                (j * cores + h, target(step, half, j, h) * cores + j // half)
                for j in range(blocks)
                for h in range(cores)
            ]
            parts.append(lax.ppermute(product, ("chan", "core"), route))
    steps = [FIRST] + [step for call in CALLS for step in call]
    arrived = dict(zip(steps, parts))
    done = ()
    for late in (False, True):
        now = [step for step in steps if (step in JOINED_LAST) == late]
        done = [join(now, place, [arrived[step] for step in now], half, done)]
    return done[0]


def solution(mesh):
    blocks, count = mesh.devices.shape
    chips = count // 2
    inner = Mesh(mesh.devices.reshape(blocks, chips, 2), ("chan", "chip", "core"))
    dft = dft_rows(chips, blocks)

    def step(records, fir_taps, plan):
        return jax.shard_map(
            on_device,
            mesh=inner,
            in_specs=(P(), P("chan", ("chip", "core")), P(), P()),
            out_specs=P(("chip", "core"), None, None, None, "chan"),
            check_vma=False,
        )(jnp.asarray(dft), records, fir_taps, plan)

    return step
```

```python
import functools
import math

import jax
import jax.numpy as jnp
import numpy as np
from jax import lax
from jax.experimental import pallas as pl
from jax.experimental.pallas import tpu as pltpu
from jax.sharding import Mesh
from jax.sharding import PartitionSpec as P

WL = 256
F = 64
TAPS = 64
ROUNDS = 2
STEP_WINDOWS = 8
PIECES = 3
TILE = 16
VMEM = 32 * 1024 * 1024
SMALL_VMEM = 8 * 1024 * 1024
FIRST = 2
CALLS = ((6, 4, 3), (7, 5), (0, 1))
JOINED_LAST = (5, 0, 1)


def dft_rows(chips, blocks):
    place = np.arange(F)
    bin_number = blocks * (place % chips) + place // chips + 1
    phase = np.arange(WL)[None, :] * bin_number[:, None] % WL * (2.0 * math.pi / WL)
    return np.concatenate([np.cos(phase), -np.sin(phase)]).astype(np.float32)


def in_pieces(table):
    pieces = []
    rest = table
    for _ in range(PIECES):
        piece = rest.astype(jnp.bfloat16).astype(jnp.float32)
        pieces.append(piece)
        rest = rest - piece
    return pieces


def table_kernel(
    taps_at, dft_at, records_ref, main_ref, before_ref, order_ref, early_ref, taps_ref, dft_ref, sems
):
    taps_copy = pltpu.make_async_copy(taps_at, taps_ref, sems.at[0])
    dft_copy = pltpu.make_async_copy(dft_at, dft_ref, sems.at[1])
    taps_copy.start()
    dft_copy.start()
    early_copy = pltpu.make_async_copy(
        records_ref.at[:, : STEP_WINDOWS * WL], early_ref, sems.at[2]
    )
    early_copy.start()
    row = lax.broadcasted_iota(jnp.int32, order_ref.shape, 0)
    column = lax.broadcasted_iota(jnp.int32, order_ref.shape, 1)
    source = (row & 7) * 32 + ((row >> 3) & 1) * 16 + (row >> 4)
    order_ref[...] = jnp.where(column == source, 1.0, 0.0).astype(jnp.bfloat16)
    taps_copy.wait()
    lane = lax.broadcasted_iota(jnp.int32, (1, 2 * WL), 1)
    reversed_taps = jnp.zeros((1, 2 * WL), jnp.float32)
    for tap in range(TAPS):
        reversed_taps = jnp.where(lane == TAPS - 1 - tap, taps_ref[tap], reversed_taps)
    spread = jnp.broadcast_to(reversed_taps, (WL, 2 * WL))
    toeplitz = pltpu.roll(spread, WL - TAPS + 1, 1, stride=1, stride_axis=0)
    dft_copy.wait()
    combined = jnp.dot(
        dft_ref[...], toeplitz, precision=lax.Precision.HIGHEST, preferred_element_type=jnp.float32
    )
    main_ref[...] = jnp.concatenate(in_pieces(combined[:, WL:]), axis=0).astype(jnp.bfloat16)
    high, middle, low = in_pieces(combined[:, WL // 2 : WL])
    left = lax.broadcasted_iota(jnp.int32, high.shape, 1) < TAPS
    first = jnp.where(left, pltpu.roll(high, TAPS, 1), middle)
    second = jnp.where(left, pltpu.roll(low, TAPS, 1), 0.0)
    before_ref[...] = jnp.concatenate([first, second], axis=1).astype(jnp.bfloat16)
    early_copy.wait()


IN_VMEM = pl.BlockSpec(memory_space=pltpu.VMEM)
IN_SMEM = pl.BlockSpec(memory_space=pltpu.SMEM)
IN_HBM = pl.BlockSpec(memory_space=pltpu.HBM)


def make_tables(fir_taps, dft, records):
    rows = (PIECES * 2 * F, 2 * F, WL)
    return pl.pallas_call(
        table_kernel,
        out_shape=[jax.ShapeDtypeStruct((count, WL), jnp.bfloat16) for count in rows]
        + [jax.ShapeDtypeStruct((records.shape[0], STEP_WINDOWS * WL), jnp.bfloat16)],
        in_specs=[IN_HBM] * 3,
        out_specs=[IN_VMEM] * 4,
        scratch_shapes=[
            pltpu.SMEM(fir_taps.shape, jnp.float32),
            pltpu.VMEM(dft.shape, jnp.float32),
            pltpu.SemaphoreType.DMA((3,)),
        ],
        compiler_params=pltpu.CompilerParams(vmem_limit_bytes=SMALL_VMEM),
        name="table",
    )(*(pltpu.with_memory_space_constraint(given, pltpu.HBM) for given in (fir_taps, dft, records)))


def last_samples(across):
    return jnp.concatenate([across[across.shape[0] - TAPS :]] * (WL // TAPS), axis=0)


def spectra_kernel(
    tail_ref,
    main_ref,
    before_ref,
    order_ref,
    early_ref,
    records_ref,
    out_ref,
    samples_ref,
    carry_ref,
    held_ref,
    white_ref,
    in_sems,
    out_sems,
):
    groups = samples_ref.shape[0] + 1
    width = STEP_WINDOWS * WL
    count = 2 * F
    before = before_ref[...]

    def fetch(group):
        source = records_ref.at[:, pl.ds(pl.multiple_of(group * width, width), width)]
        return pltpu.make_async_copy(source, samples_ref.at[group - 1], in_sems.at[group - 1])

    def rows_of(group):
        return pl.ds(pl.multiple_of(group * TILE, TILE), TILE)

    def send(group):
        at = rows_of(group)
        return pltpu.make_async_copy(white_ref.at[:, at, :], out_ref.at[:, at, :], out_sems.at[group])

    def make(samples_at):
        carry = carry_ref[...]
        for inner in range(STEP_WINDOWS):
            across = samples_at[:, inner * WL : (inner + 1) * WL].T
            rows = jnp.dot(main_ref[...], across, preferred_element_type=jnp.float32)
            stacked = rows[2 * count :] + rows[count : 2 * count] + carry + rows[:count]
            carry = jnp.dot(before, last_samples(across), preferred_element_type=jnp.float32)
            power = jnp.sum(stacked * stacked, axis=0, keepdims=True) * (1.0 / count) + 1e-06
            held_ref[inner] = (stacked * (1.0 / jnp.sqrt(power))).astype(jnp.bfloat16)
        carry_ref[...] = carry

    def place(group):
        for part in range(F // TILE):
            rows = []
            for inner in range(STEP_WINDOWS):
                for start in (part * TILE, F + part * TILE):
                    rows.append(held_ref[inner, start : start + TILE, :])
            placed = jnp.dot(
                order_ref[...], jnp.concatenate(rows, axis=0), preferred_element_type=jnp.float32
            ).astype(jnp.bfloat16)
            for n in range(TILE):
                white_ref[part * TILE + n, rows_of(group), :] = placed[n * TILE : (n + 1) * TILE]

    for group in range(1, groups):
        fetch(group).start()
    carry_ref[...] = jnp.dot(before, last_samples(tail_ref[...].T), preferred_element_type=jnp.float32)
    make(early_ref)

    @pl.loop(1, groups)
    def _(group):
        fetch(group).wait()
        place(group - 1)
        make(samples_ref.at[group - 1])
        send(group - 1).start()

    place(groups - 1)
    send(groups - 1).start()
    for group in range(groups):
        send(group).wait()


def spectra(tail, tables, records):
    channels, samples = records.shape
    groups = samples // WL // STEP_WINDOWS
    result = (F, groups * TILE, channels)
    return pl.pallas_call(
        spectra_kernel,
        out_shape=pltpu.HBM(result, jnp.bfloat16),
        in_specs=[IN_VMEM] * 5 + [IN_HBM],
        out_specs=IN_HBM,
        scratch_shapes=[
            pltpu.VMEM((groups - 1, channels, STEP_WINDOWS * WL), jnp.bfloat16),
            pltpu.VMEM((2 * F, channels), jnp.float32),
            pltpu.VMEM((STEP_WINDOWS, 2 * F, channels), jnp.bfloat16),
            pltpu.VMEM(result, jnp.bfloat16),
            pltpu.SemaphoreType.DMA((groups - 1,)),
            pltpu.SemaphoreType.DMA((groups,)),
        ],
        compiler_params=pltpu.CompilerParams(vmem_limit_bytes=VMEM),
        name="spectra",
    )(tail, *tables, pltpu.with_memory_space_constraint(records, pltpu.HBM))


def rotated(rows):
    wide = rows.astype(jnp.float32)
    layers = []
    for start in range(0, rows.shape[0], TILE):
        middle = start + TILE // 2
        layers += [wide[middle : start + TILE], -wide[start:middle]]
    return jnp.concatenate(layers, axis=0).astype(jnp.bfloat16)


TN = (((0,), (0,)), ((), ()))


def target(step, half, place, core):
    return place ^ (step // 2) ^ (half * ((step % 2) ^ core))


def cross_kernel(scale, steps, plan_ref, place_ref, here_ref, other_ref, *refs):
    half_blocks = here_ref.shape[0] // 2
    picked = other_ref.shape[0] == 2
    out_refs = refs[-len(steps) :]
    for step, out_ref in zip(steps, out_refs):
        own_at = target(step, half_blocks, place_ref[0], place_ref[1])
        mate_at = plan_ref[place_ref[1], own_at]
        own = jnp.concatenate([here_ref[own_at], other_ref[0 if picked else own_at]], axis=0)
        mate = jnp.concatenate([here_ref[mate_at], other_ref[1 if picked else mate_at]], axis=0)
        for half, rows in enumerate((own, rotated(own))):
            product = lax.dot_general(mate, rows, TN, preferred_element_type=jnp.float32) * scale
            out_ref[half] = product.astype(jnp.bfloat16)


def cross(steps, plan, place, here, other, scale):
    depth, channels = here.shape[1:]
    return pl.pallas_call(
        functools.partial(cross_kernel, scale, steps),
        in_specs=[IN_SMEM, IN_SMEM, IN_VMEM, IN_VMEM],
        out_specs=[IN_VMEM] * len(steps),
        out_shape=[jax.ShapeDtypeStruct((2, channels, channels), jnp.bfloat16)] * len(steps),
        compiler_params=pltpu.CompilerParams(vmem_limit_bytes=SMALL_VMEM),
        cost_estimate=pl.CostEstimate(
            flops=len(steps) * 2 * 2 * 2 * depth * channels * channels,
            bytes_accessed=len(steps) * (8 * depth * channels + 4 * channels * channels),
            transcendentals=0,
        ),
        name="cross",
    )(plan, place, here, other)


def join_kernel(steps, bins, place_ref, *refs):
    parts, (out_ref, wide_ref, sems) = refs[: len(steps)], refs[-3:]
    copies = []
    for n, step in enumerate(steps):
        own_bin = (place_ref[0] % bins) ^ (step // 2)
        round_index = (place_ref[0] // bins) ^ place_ref[1] ^ (step % 2)
        wide_ref[n] = parts[n][...].astype(jnp.float32)
        copy = pltpu.make_async_copy(wide_ref.at[n], out_ref.at[own_bin, round_index], sems.at[n])
        copy.start()
        copies.append(copy)
    for copy in copies:
        copy.wait()


def join(steps, place, parts, bins, earlier=()):
    halves, rows, channels = parts[0].shape
    return pl.pallas_call(
        functools.partial(join_kernel, steps, bins),
        in_specs=[IN_SMEM] + [IN_VMEM] * len(steps) + [IN_HBM] * len(earlier),
        out_specs=IN_HBM,
        out_shape=jax.ShapeDtypeStruct((bins, ROUNDS, halves, rows, channels), jnp.float32),
        scratch_shapes=[
            pltpu.VMEM((len(steps), halves, rows, channels), jnp.float32),
            pltpu.SemaphoreType.DMA((len(steps),)),
        ],
        input_output_aliases={1 + len(steps): 0} if earlier else {},
        compiler_params=pltpu.CompilerParams(vmem_limit_bytes=SMALL_VMEM),
        cost_estimate=pl.CostEstimate(
            flops=0, bytes_accessed=len(steps) * 6 * halves * rows * channels, transcendentals=0
        ),
        name="join",
    )(place, *parts, *earlier)


def on_device(dft, records, fir_taps, plan):
    channels, samples_here = records.shape
    chips = lax.axis_size("chip")
    cores = lax.axis_size("core")
    blocks = lax.axis_size("chan")
    core = lax.axis_index("core").astype(jnp.int32)
    count = chips * cores
    tail = lax.ppermute(
        records[:, samples_here - WL // 2 :], ("chip", "core"), [(i, i + 1) for i in range(count - 1)]
    )
    swap = [(0, 1), (1, 0)]
    scale = 1.0 / math.sqrt(samples_here // WL * count)
    white = spectra(tail, make_tables(fir_taps, dft, records), records)
    here = lax.all_to_all(white, ("chan", "chip"), 0, 0, tiled=True)
    here = here.reshape(blocks, chips * white.shape[1], channels)
    half = blocks // 2
    place = jnp.stack([lax.axis_index("chan").astype(jnp.int32), core])
    away_at = target(FIRST, half, place[0], 1 - core)
    away = [here[away_at], here[plan[1 - core, away_at]]]
    first_other = lax.ppermute(jnp.stack(away), "core", swap)
    here, first_other = lax.optimization_barrier((here, first_other))
    other = lax.ppermute(here, "core", swap)
    parts = []
    for call in ((FIRST,), *CALLS):
        products = cross(call, plan, place, here, first_other if call == (FIRST,) else other, scale)
        if call == (FIRST,):
            here, *products = lax.optimization_barrier((here, *products))
        else:
            here, other, *products = lax.optimization_barrier((here, other, *products))
        for step, product in zip(call, products):
            route = [
                (j * cores + h, target(step, half, j, h) * cores + j // half)
                for j in range(blocks)
                for h in range(cores)
            ]
            parts.append(lax.ppermute(product, ("chan", "core"), route))
    steps = [FIRST] + [step for call in CALLS for step in call]
    arrived = dict(zip(steps, parts))
    done = ()
    for late in (False, True):
        now = [step for step in steps if (step in JOINED_LAST) == late]
        done = [join(now, place, [arrived[step] for step in now], half, done)]
    return done[0]


def solution(mesh):
    blocks, count = mesh.devices.shape
    chips = count // 2
    inner = Mesh(mesh.devices.reshape(blocks, chips, 2), ("chan", "chip", "core"))
    dft = dft_rows(chips, blocks)

    def step(records, fir_taps, plan):
        return jax.shard_map(
            on_device,
            mesh=inner,
            in_specs=(P(), P("chan", ("chip", "core")), P(), P()),
            out_specs=P(("chip", "core"), None, None, None, "chan"),
            check_vma=False,
        )(jnp.asarray(dft), records, fir_taps, plan)

    return step
```

```python
import functools
import math

import jax
import jax.numpy as jnp
import numpy as np
from jax import lax
from jax.experimental import pallas as pl
from jax.experimental.pallas import tpu as pltpu
from jax.sharding import Mesh
from jax.sharding import PartitionSpec as P

WL = 256
F = 64
TAPS = 64
ROUNDS = 2
STEP_WINDOWS = 8
PIECES = 3
TILE = 16
VMEM = 32 * 1024 * 1024
SMALL_VMEM = 8 * 1024 * 1024
FIRST = 2
CALLS = ((6, 4, 3), (7, 5), (0, 1))
JOINED_LAST = (5, 0, 1)


def dft_rows(chips, blocks):
    place = np.arange(F)
    bin_number = blocks * (place % chips) + place // chips + 1
    phase = np.arange(WL)[None, :] * bin_number[:, None] % WL * (2.0 * math.pi / WL)
    return np.concatenate([np.cos(phase), -np.sin(phase)]).astype(np.float32)


def in_pieces(table):
    pieces = []
    rest = table
    for _ in range(PIECES):
        piece = rest.astype(jnp.bfloat16).astype(jnp.float32)
        pieces.append(piece)
        rest = rest - piece
    return pieces


def table_kernel(
    taps_at, dft_at, records_ref, main_ref, before_ref, order_ref, early_ref, taps_ref, dft_ref, sems
):
    taps_copy = pltpu.make_async_copy(taps_at, taps_ref, sems.at[0])
    dft_copy = pltpu.make_async_copy(dft_at, dft_ref, sems.at[1])
    taps_copy.start()
    dft_copy.start()
    early_copy = pltpu.make_async_copy(
        records_ref.at[:, : STEP_WINDOWS * WL], early_ref, sems.at[2]
    )
    early_copy.start()
    row = lax.broadcasted_iota(jnp.int32, order_ref.shape, 0)
    column = lax.broadcasted_iota(jnp.int32, order_ref.shape, 1)
    source = (row & 7) * 32 + ((row >> 3) & 1) * 16 + (row >> 4)
    order_ref[...] = jnp.where(column == source, 1.0, 0.0).astype(jnp.bfloat16)
    taps_copy.wait()
    lane = lax.broadcasted_iota(jnp.int32, (1, 2 * WL), 1)
    reversed_taps = jnp.zeros((1, 2 * WL), jnp.float32)
    for tap in range(TAPS):
        reversed_taps = jnp.where(lane == TAPS - 1 - tap, taps_ref[tap], reversed_taps)
    spread = jnp.broadcast_to(reversed_taps, (WL, 2 * WL))
    toeplitz = pltpu.roll(spread, WL - TAPS + 1, 1, stride=1, stride_axis=0)
    dft_copy.wait()
    combined = jnp.dot(
        dft_ref[...], toeplitz, precision=lax.Precision.HIGHEST, preferred_element_type=jnp.float32
    )
    main_ref[...] = jnp.concatenate(in_pieces(combined[:, WL:]), axis=0).astype(jnp.bfloat16)
    high, middle, low = in_pieces(combined[:, WL // 2 : WL])
    left = lax.broadcasted_iota(jnp.int32, high.shape, 1) < TAPS
    first = jnp.where(left, pltpu.roll(high, TAPS, 1), middle)
    second = jnp.where(left, pltpu.roll(low, TAPS, 1), 0.0)
    before_ref[...] = jnp.concatenate([first, second], axis=1).astype(jnp.bfloat16)
    early_copy.wait()


IN_VMEM = pl.BlockSpec(memory_space=pltpu.VMEM)
IN_SMEM = pl.BlockSpec(memory_space=pltpu.SMEM)
IN_HBM = pl.BlockSpec(memory_space=pltpu.HBM)


def make_tables(fir_taps, dft, records):
    rows = (PIECES * 2 * F, 2 * F, WL)
    return pl.pallas_call(
        table_kernel,
        out_shape=[jax.ShapeDtypeStruct((count, WL), jnp.bfloat16) for count in rows]
        + [jax.ShapeDtypeStruct((records.shape[0], STEP_WINDOWS * WL), jnp.bfloat16)],
        in_specs=[IN_HBM] * 3,
        out_specs=[IN_VMEM] * 4,
        scratch_shapes=[
            pltpu.SMEM(fir_taps.shape, jnp.float32),
            pltpu.VMEM(dft.shape, jnp.float32),
            pltpu.SemaphoreType.DMA((3,)),
        ],
        compiler_params=pltpu.CompilerParams(vmem_limit_bytes=SMALL_VMEM),
        name="table",
    )(*(pltpu.with_memory_space_constraint(given, pltpu.HBM) for given in (fir_taps, dft, records)))


def last_samples(across):
    return jnp.concatenate([across[across.shape[0] - TAPS :]] * (WL // TAPS), axis=0)


def spectra_kernel(
    tail_ref,
    main_ref,
    before_ref,
    order_ref,
    early_ref,
    records_ref,
    out_ref,
    samples_ref,
    carry_ref,
    held_ref,
    white_ref,
    in_sems,
    out_sems,
):
    groups = samples_ref.shape[0] + 1
    width = STEP_WINDOWS * WL
    count = 2 * F
    before = before_ref[...]

    def fetch(group):
        source = records_ref.at[:, pl.ds(pl.multiple_of(group * width, width), width)]
        return pltpu.make_async_copy(source, samples_ref.at[group - 1], in_sems.at[group - 1])

    def rows_of(group):
        return pl.ds(pl.multiple_of(group * TILE, TILE), TILE)

    def send(group):
        at = rows_of(group)
        return pltpu.make_async_copy(white_ref.at[:, at, :], out_ref.at[:, at, :], out_sems.at[group])

    def send_part(group, part):
        at = (pl.ds(part * TILE, TILE), rows_of(group), slice(None))
        return pltpu.make_async_copy(white_ref.at[at], out_ref.at[at], out_sems.at[group + part])

    def make(samples_at):
        carry = carry_ref[...]
        for inner in range(STEP_WINDOWS):
            across = samples_at[:, inner * WL : (inner + 1) * WL].T
            rows = jnp.dot(main_ref[...], across, preferred_element_type=jnp.float32)
            stacked = rows[2 * count :] + rows[count : 2 * count] + carry + rows[:count]
            carry = jnp.dot(before, last_samples(across), preferred_element_type=jnp.float32)
            power = jnp.sum(stacked * stacked, axis=0, keepdims=True) * (1.0 / count) + 1e-06
            held_ref[inner] = (stacked * (1.0 / jnp.sqrt(power))).astype(jnp.bfloat16)
        carry_ref[...] = carry

    def place(group, sent=False):
        for part in range(F // TILE):
            rows = []
            for inner in range(STEP_WINDOWS):
                for start in (part * TILE, F + part * TILE):
                    rows.append(held_ref[inner, start : start + TILE, :])
            placed = jnp.dot(
                order_ref[...], jnp.concatenate(rows, axis=0), preferred_element_type=jnp.float32
            ).astype(jnp.bfloat16)
            for n in range(TILE):
                white_ref[part * TILE + n, rows_of(group), :] = placed[n * TILE : (n + 1) * TILE]
            if sent:
                send_part(group, part).start()

    for group in range(1, groups):
        fetch(group).start()
    carry_ref[...] = jnp.dot(before, last_samples(tail_ref[...].T), preferred_element_type=jnp.float32)
    make(early_ref)

    @pl.loop(1, groups)
    def _(group):
        fetch(group).wait()
        place(group - 1)
        make(samples_ref.at[group - 1])
        send(group - 1).start()

    place(groups - 1, sent=True)
    for group in range(groups - 1):
        send(group).wait()
    for part in range(F // TILE):
        send_part(groups - 1, part).wait()


def spectra(tail, tables, records):
    channels, samples = records.shape
    groups = samples // WL // STEP_WINDOWS
    result = (F, groups * TILE, channels)
    return pl.pallas_call(
        spectra_kernel,
        out_shape=pltpu.HBM(result, jnp.bfloat16),
        in_specs=[IN_VMEM] * 5 + [IN_HBM],
        out_specs=IN_HBM,
        scratch_shapes=[
            pltpu.VMEM((groups - 1, channels, STEP_WINDOWS * WL), jnp.bfloat16),
            pltpu.VMEM((2 * F, channels), jnp.float32),
            pltpu.VMEM((STEP_WINDOWS, 2 * F, channels), jnp.bfloat16),
            pltpu.VMEM(result, jnp.bfloat16),
            pltpu.SemaphoreType.DMA((groups - 1,)),
            pltpu.SemaphoreType.DMA((groups - 1 + F // TILE,)),
        ],
        compiler_params=pltpu.CompilerParams(vmem_limit_bytes=VMEM),
        name="spectra",
    )(tail, *tables, pltpu.with_memory_space_constraint(records, pltpu.HBM))


def rotated(rows):
    wide = rows.astype(jnp.float32)
    layers = []
    for start in range(0, rows.shape[0], TILE):
        middle = start + TILE // 2
        layers += [wide[middle : start + TILE], -wide[start:middle]]
    return jnp.concatenate(layers, axis=0).astype(jnp.bfloat16)


TN = (((0,), (0,)), ((), ()))


def target(step, half, place, core):
    return place ^ (step // 2) ^ (half * ((step % 2) ^ core))


def cross_kernel(scale, steps, plan_ref, place_ref, here_ref, other_ref, *refs):
    half_blocks = here_ref.shape[0] // 2
    picked = other_ref.shape[0] == 2
    out_refs = refs[-len(steps) :]
    for step, out_ref in zip(steps, out_refs):
        own_at = target(step, half_blocks, place_ref[0], place_ref[1])
        mate_at = plan_ref[place_ref[1], own_at]
        own = jnp.concatenate([here_ref[own_at], other_ref[0 if picked else own_at]], axis=0)
        mate = jnp.concatenate([here_ref[mate_at], other_ref[1 if picked else mate_at]], axis=0)
        for half, rows in enumerate((own, rotated(own))):
            product = lax.dot_general(mate, rows, TN, preferred_element_type=jnp.float32) * scale
            out_ref[half] = product.astype(jnp.bfloat16)


def cross(steps, plan, place, here, other, scale):
    depth, channels = here.shape[1:]
    return pl.pallas_call(
        functools.partial(cross_kernel, scale, steps),
        in_specs=[IN_SMEM, IN_SMEM, IN_VMEM, IN_VMEM],
        out_specs=[IN_VMEM] * len(steps),
        out_shape=[jax.ShapeDtypeStruct((2, channels, channels), jnp.bfloat16)] * len(steps),
        compiler_params=pltpu.CompilerParams(vmem_limit_bytes=SMALL_VMEM),
        cost_estimate=pl.CostEstimate(
            flops=len(steps) * 2 * 2 * 2 * depth * channels * channels,
            bytes_accessed=len(steps) * (8 * depth * channels + 4 * channels * channels),
            transcendentals=0,
        ),
        name="cross",
    )(plan, place, here, other)


def join_kernel(steps, bins, place_ref, *refs):
    parts, (out_ref, wide_ref, sems) = refs[: len(steps)], refs[-3:]
    copies = []
    for n, step in enumerate(steps):
        own_bin = (place_ref[0] % bins) ^ (step // 2)
        round_index = (place_ref[0] // bins) ^ place_ref[1] ^ (step % 2)
        wide_ref[n] = parts[n][...].astype(jnp.float32)
        copy = pltpu.make_async_copy(wide_ref.at[n], out_ref.at[own_bin, round_index], sems.at[n])
        copy.start()
        copies.append(copy)
    for copy in copies:
        copy.wait()


def join(steps, place, parts, bins, earlier=()):
    halves, rows, channels = parts[0].shape
    return pl.pallas_call(
        functools.partial(join_kernel, steps, bins),
        in_specs=[IN_SMEM] + [IN_VMEM] * len(steps) + [IN_HBM] * len(earlier),
        out_specs=IN_HBM,
        out_shape=jax.ShapeDtypeStruct((bins, ROUNDS, halves, rows, channels), jnp.float32),
        scratch_shapes=[
            pltpu.VMEM((len(steps), halves, rows, channels), jnp.float32),
            pltpu.SemaphoreType.DMA((len(steps),)),
        ],
        input_output_aliases={1 + len(steps): 0} if earlier else {},
        compiler_params=pltpu.CompilerParams(vmem_limit_bytes=SMALL_VMEM),
        cost_estimate=pl.CostEstimate(
            flops=0, bytes_accessed=len(steps) * 6 * halves * rows * channels, transcendentals=0
        ),
        name="join",
    )(place, *parts, *earlier)


def on_device(dft, records, fir_taps, plan):
    channels, samples_here = records.shape
    chips = lax.axis_size("chip")
    cores = lax.axis_size("core")
    blocks = lax.axis_size("chan")
    core = lax.axis_index("core").astype(jnp.int32)
    count = chips * cores
    tail = lax.ppermute(
        records[:, samples_here - WL // 2 :], ("chip", "core"), [(i, i + 1) for i in range(count - 1)]
    )
    swap = [(0, 1), (1, 0)]
    scale = 1.0 / math.sqrt(samples_here // WL * count)
    white = spectra(tail, make_tables(fir_taps, dft, records), records)
    here = lax.all_to_all(white, ("chan", "chip"), 0, 0, tiled=True)
    here = here.reshape(blocks, chips * white.shape[1], channels)
    half = blocks // 2
    place = jnp.stack([lax.axis_index("chan").astype(jnp.int32), core])
    away_at = target(FIRST, half, place[0], 1 - core)
    away = [here[away_at], here[plan[1 - core, away_at]]]
    first_other = lax.ppermute(jnp.stack(away), "core", swap)
    here, first_other = lax.optimization_barrier((here, first_other))
    other = lax.ppermute(here, "core", swap)
    parts = []
    for call in ((FIRST,), *CALLS):
        products = cross(call, plan, place, here, first_other if call == (FIRST,) else other, scale)
        if call == (FIRST,):
            here, *products = lax.optimization_barrier((here, *products))
        else:
            here, other, *products = lax.optimization_barrier((here, other, *products))
        for step, product in zip(call, products):
            route = [
                (j * cores + h, target(step, half, j, h) * cores + j // half)
                for j in range(blocks)
                for h in range(cores)
            ]
            parts.append(lax.ppermute(product, ("chan", "core"), route))
    steps = [FIRST] + [step for call in CALLS for step in call]
    arrived = dict(zip(steps, parts))
    done = ()
    for late in (False, True):
        now = [step for step in steps if (step in JOINED_LAST) == late]
        done = [join(now, place, [arrived[step] for step in now], half, done)]
    return done[0]


def solution(mesh):
    blocks, count = mesh.devices.shape
    chips = count // 2
    inner = Mesh(mesh.devices.reshape(blocks, chips, 2), ("chan", "chip", "core"))
    dft = dft_rows(chips, blocks)

    def step(records, fir_taps, plan):
        return jax.shard_map(
            on_device,
            mesh=inner,
            in_specs=(P(), P("chan", ("chip", "core")), P(), P()),
            out_specs=P(("chip", "core"), None, None, None, "chan"),
            check_vma=False,
        )(jnp.asarray(dft), records, fir_taps, plan)

    return step
```
